256 devices in a mesh: lat: 64 (over z_lo, x, y, core), ch: 4 (over z_hi).
Axes of the slice: x: 4, y: 4, z: 8 (z_hi: 4, z_lo: 2; z = z_hi * 2 + z_lo), core: 2. Of those that a mesh axis runs over, the one named last changes fastest.
Arguments:
- x_field: bfloat16 [192, 256, 1440], P('lat', 'ch'), may hold values from -16 to 16
- cotangent: bfloat16 [192, 256, 1440], P('lat', 'ch'), may hold values from -6 to 6
- halo_rows: int32 [192, 5], P('lat'), may hold values from -1 to 191, as said below
- filters: bfloat16 [192, 5, 9, 16], P('lat'), may hold values from -0.625 to 0.625
- mixing: bfloat16 [9, 256, 256], replicated, may hold values from -0.125 to 0.125
Outputs:
- y_field: bfloat16 [192, 256, 1440], P('lat', 'ch')
- x_grad: bfloat16 [192, 256, 1440], P('lat', 'ch')
- w_grad: float32 [256, 9, 256], P('lat', None, 'ch')
The draws below stay inside these ranges and needn't reach their ends.
Inputs may be any that keep to these rules, and one draw needn't show every extreme that they name: The entries of halo_rows[i] other than -1 are distinct latitudes within 2 of i, and always include i - 1, i and i + 1 where these lie in the grid; their order among the slots is arbitrary.
All inputs are finite; a program needn't handle non-finite values.
Results may differ from the reference program's by a relative error of at most 0.006.
Values may be sent and summed in bfloat16 or wider, within the bound.
No kernel may reach another device: no remote copies, remote signals or barrier semaphores. Data moves between devices by JAX's collectives and lax.ppermute only.
A program may use at most 128 MiB of HBM per device.

```python
import math
import jax
import jax.numpy as jnp
from jax import lax

C = 256
NLON = 1440
K = 9
HALF = 2
LW = 16
ROWS_DEV = 3
SLOTS = 5
NLAT = 192


def draw_halo_rows(key, part):
    key = jax.random.fold_in(key, 7)
    far_key, order_key = jax.random.split(key)
    latitude = jnp.arange(NLAT, dtype=jnp.int32)[:, None]
    offsets = jnp.arange(SLOTS, dtype=jnp.int32)[None, :] - HALF
    target = latitude + offsets
    near = jnp.abs(offsets) <= 1
    keep_far = jax.random.randint(far_key, (NLAT, SLOTS), 0, 4) != 0
    inside = (target >= 0) & (target < NLAT)
    valid = (near | keep_far) & inside
    entries = jnp.where(valid, target, -1).astype(jnp.int32)
    scores = jax.random.randint(order_key, (NLAT, SLOTS), 0, 1 << 20) * SLOTS + jnp.arange(SLOTS, dtype=jnp.int32)[None, :]
    order = jnp.argsort(scores, axis=1)
    return jnp.take_along_axis(entries, order, axis=1).astype(jnp.int32)


def spiked(result, own_key, source, target, blocks, factor):
    def block_of(position):
        return (jnp.arange(result.shape[position]) // (result.shape[position] // blocks)).reshape((-1,) + (1,) * (result.ndim - 1 - position))

    first = jax.random.permutation(own_key, blocks)[block_of(target)]
    second = (block_of(target) + blocks // 2) % blocks
    return jnp.where((block_of(source) == first) | (block_of(source) == second), factor * result, result)


def block_scale(stream_key, extent, cuts, smallest, top_value):
    def one(position, shards_of):
        steps = jax.random.uniform(jax.random.fold_in(jax.random.fold_in(stream_key, 6), position), (shards_of,), jnp.float32, smallest / len(cuts), top_value / len(cuts))
        return jnp.repeat(jnp.exp(steps), extent[position] // shards_of).reshape((-1,) + (1,) * (len(extent) - position - 1))

    loudness = one(*cuts[0])
    for cut in cuts[1:]:
        loudness = loudness * one(*cut)
    return loudness


def gaussian(rng, extent, scale, reach, shards=(), kind=jnp.bfloat16):
    result = jax.random.normal(rng, extent, jnp.float32) * scale
    if len(shards) > 0:
        result = block_scale(rng, extent, shards, -0.22, 0.18) * result
    return jnp.clip(result, min=-reach, max=reach).astype(kind)


def heavy_noise(own_key, dims, scale, reach, cuts, heavy, kind=jnp.bfloat16):
    drawn = scale * jax.random.normal(own_key, dims, jnp.float32)
    if cuts:
        drawn = drawn * block_scale(own_key, dims, cuts, -0.22, 0.18)
    return jnp.clip(spiked(drawn, jax.random.fold_in(own_key, 3), *heavy), -reach, reach).astype(kind)


def setup_inputs(seed: int = 0) -> dict:
    keys = jax.random.split(jax.random.key(seed), 6)
    x_field = heavy_noise(keys[0], (NLAT, C, NLON), 1.0, 16.0, ((0, 64), (1, 4)), (0, 1, 64, 4.0))
    cotangent = gaussian(keys[1], (NLAT, C, NLON), 1.0, 6.0, ((0, 64), (1, 4)))
    halo_rows = draw_halo_rows(jax.random.fold_in(keys[5], 71), 0)
    filters = gaussian(keys[3], (NLAT, SLOTS, K, LW), (SLOTS * LW) ** -0.5, 0.625, ((0, 64),))
    mixing = gaussian(keys[4], (K, C, C), (K * C) ** -0.5, 0.125)
    return dict(x_field=x_field, cotangent=cotangent, halo_rows=halo_rows, filters=filters, mixing=mixing)


def build_taps(rows_block, filt_block, base, count):
    hit = (rows_block[:, :, None] - base == jnp.arange(count, dtype=jnp.int32)[None, None, :]).astype(jnp.float32)
    taps = jnp.einsum('irs,irkl->iksl', hit, filt_block.astype(jnp.float32))
    return taps.reshape(rows_block.shape[0] * K, count, LW)

def spread(field, taps):
    front = LW // 2
    back = LW - 1 - front
    padded = jnp.concatenate([field[:, :, NLON - front:], field, field[:, :, :back]], axis=2)
    return lax.conv_general_dilated(padded, taps, (1,), 'VALID', dimension_numbers=('CNH', 'OIH', 'CNH'), precision=lax.Precision.HIGHEST, preferred_element_type=jnp.float32)

def collect(grad, taps):
    front = LW - 1 - LW // 2
    back = LW // 2
    padded = jnp.concatenate([grad[:, :, NLON - front:], grad, grad[:, :, :back]], axis=2)
    return lax.conv_general_dilated(padded, taps[:, :, ::-1], (1,), 'VALID', dimension_numbers=('CNH', 'IOH', 'CNH'), precision=lax.Precision.HIGHEST, preferred_element_type=jnp.float32)

def reference(x_field, cotangent, halo_rows, filters, mixing):
    span = ROWS_DEV + 2 * HALF
    padded_x = jnp.pad(x_field.astype(jnp.float32), ((HALF, HALF), (0, 0), (0, 0)))
    weights = mixing.astype(jnp.float32)

    def step(carry, block):
        weight_total, grad_total = carry
        start = (block * ROWS_DEV).astype(jnp.int32)
        window = lax.dynamic_slice_in_dim(padded_x, start, span, 0)
        rows_block = lax.dynamic_slice_in_dim(halo_rows, start, ROWS_DEV, 0)
        filt_block = lax.dynamic_slice_in_dim(filters, start, ROWS_DEV, 0)
        taps = build_taps(rows_block, filt_block, start - HALF, span)
        basis = lax.optimization_barrier(spread(window, taps).astype(jnp.bfloat16)).astype(jnp.float32)
        basis = basis.reshape(ROWS_DEV, K, C, NLON)
        y_block = jnp.einsum('ikcj,kco->ioj', basis, weights, precision=lax.Precision.HIGHEST).astype(jnp.bfloat16)
        grad_block = lax.dynamic_slice_in_dim(cotangent, start, ROWS_DEV, 0).astype(jnp.float32)
        basis_grad = jnp.einsum('ioj,kco->ikcj', grad_block, weights, precision=lax.Precision.HIGHEST)
        basis_grad = lax.optimization_barrier(basis_grad.astype(jnp.bfloat16)).astype(jnp.float32)
        weight_term = jnp.einsum('ikcj,ioj->cko', basis, grad_block, precision=lax.Precision.HIGHEST)
        partial_grad = collect(basis_grad.reshape(ROWS_DEV * K, C, NLON), taps)
        current = lax.dynamic_slice_in_dim(grad_total, start, span, 0)
        grad_total = lax.dynamic_update_slice_in_dim(grad_total, current + partial_grad, start, 0)
        return ((weight_total + weight_term, grad_total), y_block)
    start_carry = (jnp.zeros((C, K, C), jnp.float32), jnp.zeros((NLAT + 2 * HALF, C, NLON), jnp.float32))
    blocks = jnp.arange(NLAT // ROWS_DEV, dtype=jnp.int32)
    (weight_total, grad_total), y_blocks = lax.scan(step, start_carry, blocks)
    y_field = y_blocks.reshape(NLAT, C, NLON)
    x_grad = grad_total[HALF:HALF + NLAT].astype(jnp.bfloat16)
    w_grad = weight_total * (1.0 / math.sqrt(NLAT * NLON))
    return (y_field, x_grad, w_grad)
```

```python
import functools
import math

import jax
import jax.numpy as jnp
from jax import lax
from jax.experimental import pallas as pl
from jax.experimental.pallas import tpu as pltpu
from jax.sharding import PartitionSpec as P

BF = jnp.bfloat16
F32 = jnp.float32
ROWS = 3
OWN = 64
C = 256
J = 1440
K = 9
PART = 360
WIN = 384
PAD = 400
BLK = 32
SPAN = 48
REACH = 2
NSP = 5
X_OFF = 16
G_OFF = 8
VMEM_LIMIT = 56 * 1024 * 1024

VM = pl.BlockSpec(memory_space=pltpu.VMEM)
SM = pl.BlockSpec(memory_space=pltpu.SMEM)


def call(body, name, outs, n_in, scratch=(), flops=0, nbytes=0):
    return pl.pallas_call(
        body,
        out_shape=[jax.ShapeDtypeStruct(s, d) for s, d in outs],
        in_specs=[SM] + [VM] * n_in,
        out_specs=[VM] * len(outs),
        scratch_shapes=list(scratch),
        compiler_params=pltpu.CompilerParams(vmem_limit_bytes=VMEM_LIMIT),
        cost_estimate=pl.CostEstimate(flops=flops, bytes_accessed=nbytes, transcendentals=0),
        name=name,
    )


def pick4(value):
    return lax.rem(value + 4, 4)


def pack_body(off, idx, x, o0, o1, o2, o3, win):
    ch = idx[0]
    for r in range(ROWS):
        v = x[r]
        for h in range(4):
            a = PART * h - off
            if a < 0:
                w = jnp.concatenate([v[:, J + a :], v[:, : WIN + a]], axis=1)
            elif a + WIN > J:
                w = jnp.concatenate([v[:, a:], v[:, : a + WIN - J]], axis=1)
            else:
                w = v[:, a : a + WIN]
            win[h, r] = w
    for s, o in enumerate((o0, o1, o2, o3)):
        o[...] = win[pick4(ch + s)]


def gather_parts(ch, refs, scr):
    for s, ref in enumerate(refs):
        src = pick4(ch - s)
        scr[:, pl.ds(pl.multiple_of(src * OWN, OWN), OWN), :] = ref[...]


def asm_x_body(idx, p0, p1, p2, p3, out, head, tail, scr):
    gather_parts(idx[0], (p0, p1, p2, p3), scr)
    zeros = jnp.zeros((PAD - WIN, C), BF)
    for r in range(ROWS):
        t = scr[r].T
        for dst, pos in ((out, r), (head, r), (tail, r - 1)):
            if 0 <= pos < dst.shape[0]:
                dst[pos, :WIN, :] = t
                dst[pos, WIN:, :] = zeros


def asm_g_body(idx, p0, p1, p2, p3, out, out_t, scr):
    gather_parts(idx[0], (p0, p1, p2, p3), scr)
    lane = lax.broadcasted_iota(jnp.int32, (C, WIN), 1)
    own = (lane >= G_OFF) & (lane < G_OFF + PART)
    for r in range(ROWS):
        v = scr[r]
        out[r] = v.T
        out_t[r] = jnp.where(own, v.astype(F32), 0.0).astype(BF)


def bands_body(idx, a, b, ta, tb):
    for n in range(ROWS * K):
        i, k = divmod(n, K)
        row = jnp.broadcast_to(a[n : n + 1, :], (BLK, 256))
        ta[i, k * BLK : (k + 1) * BLK, :] = pltpu.roll(row, 0, 1, stride=1, stride_axis=0).astype(BF)
    for n in range(ROWS * NSP):
        i, sp = divmod(n, NSP)
        row = jnp.broadcast_to(b[n : n + 1, :], (BLK, 512))
        tb[i, sp * BLK : (sp + 1) * BLK, :] = pltpu.roll(row, 0, 1, stride=1, stride_axis=0).astype(BF)


def forward_body(idx, x, xp, xn, ta, gt, mix, y0, y1, y2, y3, keep, send, basis, yt):
    ch = idx[0]
    core = idx[1]
    rows = [xp.at[0], xp.at[1], x.at[0], x.at[1], x.at[2], xn.at[0], xn.at[1]]
    zeros = jnp.zeros((256 - NSP * SPAN, C), BF)

    @pl.loop(0, WIN // BLK)
    def _(b):
        at = pl.multiple_of(b * BLK, BLK)
        for i in range(ROWS):
            rhs = jnp.concatenate([rows[i + sp][pl.ds(at, SPAN), :] for sp in range(NSP)] + [zeros], axis=0)
            out = jnp.dot(ta[i], rhs, preferred_element_type=F32).astype(BF)
            for k in range(K):
                basis[pl.ds(pl.multiple_of(i * WIN + at, BLK), BLK), k * C : (k + 1) * C] = out[k * BLK : (k + 1) * BLK]

    m = mix[...]
    for i in range(ROWS):
        y = jnp.dot(basis[i * WIN : (i + 1) * WIN, :], m, preferred_element_type=F32)
        yt[i] = y.T.astype(BF)
    for s, o in enumerate((y0, y1, y2, y3)):
        o[...] = yt[:, pl.ds(pl.multiple_of(pick4(ch + s) * OWN, OWN), OWN), :]

    g = jnp.concatenate([gt[i] for i in range(ROWS)], axis=1)
    low = lax.broadcasted_iota(jnp.int32, (16, 8, C), 1) < 4
    first = core == 0
    for k in range(K):
        w = jnp.dot(g, basis[:, k * C : (k + 1) * C], preferred_element_type=F32).T
        t = w.reshape(2, 16, 8, C)
        even = jnp.where(low, t[0], pltpu.roll(t[1], 4, 1))
        odd = jnp.where(low, pltpu.roll(t[0], 4, 1), t[1])
        keep[:, 8 * k : 8 * k + 8, :] = jnp.where(first, even, odd)
        send[:, 8 * k : 8 * k + 8, :] = jnp.where(first, odd, even)


def backward_body(idx, g, tb, mix, mid, lower, upper, bg):
    bg[:, WIN:, :] = jnp.zeros((ROWS, PAD - WIN, K * C), BF)
    for i in range(ROWS):
        for k in range(K):
            bg[i, :WIN, k * C : (k + 1) * C] = lax.dot_general(
                g[i], mix[k * C : (k + 1) * C, :], (((1,), (1,)), ((), ())), preferred_element_type=F32
            ).astype(BF)
    zeros = jnp.zeros((512 - K * SPAN, C), BF)

    @pl.loop(0, WIN // BLK)
    def _(b):
        at = pl.multiple_of(b * BLK, BLK)
        acc = [None] * (ROWS + 2 * REACH)
        for i in range(ROWS):
            rhs = jnp.concatenate(
                [bg[i, pl.ds(at, SPAN), k * C : (k + 1) * C] for k in range(K)] + [zeros], axis=0
            )
            out = jnp.dot(tb[i], rhs, preferred_element_type=F32)
            for sp in range(NSP):
                part = out[sp * BLK : (sp + 1) * BLK]
                acc[i + sp] = part if acc[i + sp] is None else acc[i + sp] + part
        for n in range(2):
            lower[n, pl.ds(at, BLK), :] = acc[n].astype(BF)
            upper[n, pl.ds(at, BLK), :] = acc[ROWS + REACH + n].astype(BF)
        for n in range(ROWS):
            mid[n, pl.ds(at, BLK), :] = acc[REACH + n]


def join_body(idx, mid, prev, after, o0, o1, o2, o3, scr):
    ch = idx[0]
    for r in range(ROWS):
        v = mid[r]
        if r < REACH:
            v = v + prev[r].astype(F32)
        if r >= ROWS - REACH:
            v = v + after[r - (ROWS - REACH)].astype(F32)
        scr[r] = v.T.astype(BF)
    for s, o in enumerate((o0, o1, o2, o3)):
        o[...] = scr[:, pl.ds(pl.multiple_of(pick4(ch + s) * OWN, OWN), OWN), :]


def unpack_body(off, idx, p0, p1, p2, p3, out, scr):
    for s, ref in enumerate((p0, p1, p2, p3)):
        scr[pick4(idx[0] - s)] = ref[...]
    for r in range(ROWS):
        out[r] = jnp.concatenate([scr[h, r][:, off : off + PART] for h in range(4)], axis=1)


def fold_y_body(idx, keep, got, own, o1, o2, o3):
    for s, o in enumerate((own, o1, o2, o3)):
        t = pick4(idx[2] + s)
        for x in range(4):
            v = keep[x * 4 + t] + got[x * 4 + t]
            o[x * 72 : (x + 1) * 72, :] = v.astype(o.dtype)


def fold_x_body(idx, own, r1, r2, r3, o0, o1, o2, o3, scr):
    total = own[...] + r1[...].astype(F32) + r2[...].astype(F32) + r3[...].astype(F32)
    scr[...] = total.reshape(4, 72, C)
    for s, o in enumerate((o0, o1, o2, o3)):
        o[...] = scr[pick4(idx[3] + s)]


def fold_ch_body(idx, own, r1, r2, r3, o0, o1, o2, o3, scr):
    total = own[...] + r1[...] + r2[...] + r3[...]
    for h in range(4):
        scr[h] = total[:, h * OWN : (h + 1) * OWN]
    for s, o in enumerate((o0, o1, o2, o3)):
        o[...] = scr[pick4(idx[0] + s)]


def fold_z_body(idx, own, r1, r2, r3, out):
    out[...] = own[...] + r1[...] + r2[...] + r3[...]


def ring_ch(step):
    return [(i, (i + step) % 4) for i in range(4)]


def ring_lat(place, step):
    out = []
    for i in range(64):
        digit = i // place % 4
        out.append((i, i + ((digit + step) % 4 - digit) * place))
    return out


def local(x_field, cotangent, halo_rows, filters, mixing):
    lat = lax.axis_index("lat")
    ch = lax.axis_index("ch")
    idx = jnp.stack([ch, lat % 2, lat // 2 % 4, lat // 8 % 4]).astype(jnp.int32)
    mix2 = mixing.reshape(K * C, C)
    part = ((ROWS, OWN, WIN), BF)

    def exchange(parts):
        return [parts[0]] + [lax.ppermute(parts[s], "ch", ring_ch(s)) for s in (1, 2, 3)]

    def packed(value, off, name):
        return call(
            functools.partial(pack_body, off), name, [part] * 4, 1, [pltpu.VMEM((4, ROWS, OWN, WIN), BF)]
        )(idx, value)

    x_parts = exchange(packed(x_field, X_OFF, "pack_x"))
    g_parts = exchange(packed(cotangent, G_OFF, "pack_g"))

    want = lat * ROWS + jnp.arange(ROWS, dtype=jnp.int32)[:, None] - REACH + jnp.arange(NSP, dtype=jnp.int32)[None, :]
    hit = (halo_rows[:, :, None] == want[:, None, :]) & (halo_rows[:, :, None] >= 0)
    taps = jnp.sum(jnp.where(hit[:, :, None, :, None], filters.astype(F32)[:, :, :, None, :], 0.0), axis=1)
    ntap = taps.shape[-1]
    a = jnp.pad(taps, ((0, 0),) * 3 + ((0, SPAN - ntap),)).reshape(ROWS * K, NSP * SPAN)
    a = jnp.pad(a, ((0, 0), (0, 256 - NSP * SPAN)))
    b = jnp.pad(taps[..., ::-1], ((0, 0),) * 3 + ((1, SPAN - ntap - 1),))
    b = jnp.transpose(b, (0, 2, 1, 3)).reshape(ROWS * NSP, K * SPAN)
    b = jnp.pad(b, ((0, 0), (0, 512 - K * SPAN)))
    ta, tb = call(
        bands_body, "bands", [((ROWS, K * BLK, 256), BF), ((ROWS, NSP * BLK, 512), BF)], 2
    )(idx, a, b)

    lon = (ROWS, PAD, C)
    rim = (REACH, PAD, C)
    x_lon, x_head, x_tail = call(
        asm_x_body, "asm_x", [(lon, BF), (rim, BF), (rim, BF)], 4, [pltpu.VMEM((ROWS, C, WIN), BF)]
    )(idx, *x_parts)
    up = [(i, i + 1) for i in range(63)]
    down = [(i + 1, i) for i in range(63)]
    x_prev = lax.ppermute(x_tail, "lat", up)
    x_next = lax.ppermute(x_head, "lat", down)

    g_lon, g_t = call(
        asm_g_body,
        "asm_g",
        [((ROWS, WIN, C), BF), ((ROWS, C, WIN), BF)],
        4,
        [pltpu.VMEM((ROWS, C, WIN), BF)],
    )(idx, *g_parts)

    *y_parts, keep, send = call(
        forward_body,
        "forward",
        [part] * 4 + [((16, 72, C), F32)] * 2,
        6,
        [pltpu.VMEM((ROWS * WIN, K * C), BF), pltpu.VMEM((ROWS, C, WIN), BF)],
        flops=6_000_000_000,
        nbytes=8_000_000,
    )(idx, x_lon, x_prev, x_next, ta, g_t, mix2)
    got = lax.ppermute(send, "lat", [(i, i ^ 1) for i in range(64)])
    y_parts = exchange(y_parts)

    mid, lower, upper = call(
        backward_body,
        "backward",
        [((ROWS, WIN, C), F32), ((REACH, WIN, C), BF), ((REACH, WIN, C), BF)],
        3,
        [pltpu.VMEM((ROWS, PAD, K * C), BF)],
        flops=4_000_000_000,
        nbytes=8_000_000,
    )(idx, g_lon, tb, mix2)
    from_prev = lax.ppermute(upper, "lat", up)
    from_next = lax.ppermute(lower, "lat", down)

    own, s1, s2, s3 = call(
        fold_y_body, "fold_y", [((288, C), F32)] + [((288, C), BF)] * 3, 2
    )(idx, keep, got)
    r = [lax.ppermute(v, "lat", ring_lat(2, s)) for s, v in ((1, s1), (2, s2), (3, s3))]
    own, s1, s2, s3 = call(
        fold_x_body, "fold_x", [((72, C), F32)] * 4, 4, [pltpu.VMEM((4, 72, C), F32)]
    )(idx, own, *r)
    r = [lax.ppermute(v, "lat", ring_lat(8, s)) for s, v in ((1, s1), (2, s2), (3, s3))]
    own, s1, s2, s3 = call(
        fold_ch_body, "fold_ch", [((72, OWN), F32)] * 4, 4, [pltpu.VMEM((4, 72, OWN), F32)]
    )(idx, own, *r)
    r = [lax.ppermute(v, "ch", ring_ch(s)) for s, v in ((1, s1), (2, s2), (3, s3))]
    (half,) = call(fold_z_body, "fold_z", [((72, OWN), F32)], 4)(idx, own, *r)
    other = lax.ppermute(half, "lat", [(i, i ^ 32) for i in range(64)])
    both = ((half + other) * (1.0 / math.sqrt(64 * ROWS * J))).reshape(K, 2, 4, OWN)
    w_grad = jnp.transpose(lax.dynamic_index_in_dim(both, lat // 32, 1, keepdims=False), (1, 0, 2))

    g_out = call(join_body, "join", [part] * 4, 3, [pltpu.VMEM((ROWS, C, WIN), BF)])(
        idx, mid, from_prev, from_next
    )
    g_out = exchange(g_out)

    def unpacked(parts, off, name):
        (out,) = call(
            functools.partial(unpack_body, off),
            name,
            [((ROWS, OWN, J), BF)],
            4,
            [pltpu.VMEM((4, ROWS, OWN, WIN), BF)],
        )(idx, *parts)
        return out

    y_field = unpacked(y_parts, G_OFF, "unpack_y")
    x_grad = unpacked(g_out, 0, "unpack_g")
    return (y_field, x_grad, w_grad)


def solution(mesh):
    return jax.shard_map(
        local,
        mesh=mesh,
        in_specs=(
            P("lat", "ch", None),
            P("lat", "ch", None),
            P("lat", None),
            P("lat", None, None, None),
            P(),
        ),
        out_specs=(P("lat", "ch", None), P("lat", "ch", None), P("lat", None, "ch")),
        check_vma=False,
    )
```

```python
import functools
import math

import jax
import jax.numpy as jnp
from jax import lax
from jax.experimental import pallas as pl
from jax.experimental.pallas import tpu as pltpu
from jax.sharding import PartitionSpec as P

BF = jnp.bfloat16
F32 = jnp.float32
ROWS = 3
OWN = 64
C = 256
J = 1440
K = 9
PART = 360
WIN = 384
PAD = 400
BLK = 32
SPAN = 48
REACH = 2
NSP = 5
X_OFF = 16
G_OFF = 8
LATE = 1
MIB = 1024 * 1024

VM = pl.BlockSpec(memory_space=pltpu.VMEM)
SM = pl.BlockSpec(memory_space=pltpu.SMEM)


def call(body, name, outs, n_in, scratch=(), limit=8, flops=0, nbytes=1_000_000):
    return pl.pallas_call(
        body,
        out_shape=[jax.ShapeDtypeStruct(s, d) for s, d in outs],
        in_specs=[SM] + [VM] * n_in,
        out_specs=[VM] * len(outs),
        scratch_shapes=list(scratch),
        compiler_params=pltpu.CompilerParams(vmem_limit_bytes=limit * MIB),
        cost_estimate=pl.CostEstimate(flops=flops, bytes_accessed=nbytes, transcendentals=0),
        name=name,
    )


def pack_body(idx, g, x, o0, o1, o2, o3, win):
    for r in range(2 * ROWS):
        v = g[r] if r < ROWS else x[r - ROWS]
        for h in range(4):
            a = PART * h - (G_OFF if r < ROWS else X_OFF)
            if a < 0:
                w = jnp.concatenate([v[:, J + a :], v[:, : WIN + a]], axis=1)
            elif a + WIN > J:
                w = jnp.concatenate([v[:, a:], v[:, : a + WIN - J]], axis=1)
            else:
                w = v[:, a : a + WIN]
            win[h, r] = w
    for s, o in enumerate((o0, o1, o2, o3)):
        o[...] = win[lax.bitwise_xor(idx[0], jnp.int32(s))]


def gather_parts(ch, refs, first, scr):
    for s, ref in enumerate(refs):
        src = lax.bitwise_xor(ch, jnp.int32(s))
        scr[:, pl.ds(pl.multiple_of(src * OWN, OWN), OWN), :] = ref[first : first + ROWS]


def asm_x_body(idx, p0, p1, p2, p3, out, near, far, scr):
    gather_parts(idx[0], (p0, p1, p2, p3), ROWS, scr)
    zeros = jnp.zeros((PAD - WIN, C), BF)
    for r in range(ROWS):
        out[r, :WIN, :] = scr[r].T
        out[r, WIN:, :] = zeros

    @pl.when(idx[1] == 0)
    def _():
        near[...] = out[1:]
        far[...] = out[:REACH]

    @pl.when(idx[1] != 0)
    def _():
        near[...] = out[:REACH]
        far[...] = out[1:]


def bands_body(idx, a, b, ta, tb):
    for n in range(ROWS * K):
        i, k = divmod(n, K)
        row = jnp.broadcast_to(a[n : n + 1, :], (BLK, 256))
        ta[i, k * BLK : (k + 1) * BLK, :] = pltpu.roll(row, 0, 1, stride=1, stride_axis=0).astype(BF)
    for n in range(ROWS * NSP):
        i, sp = divmod(n, NSP)
        row = jnp.broadcast_to(b[n : n + 1, :], (BLK, 512))
        tb[i, sp * BLK : (sp + 1) * BLK, :] = pltpu.roll(row, 0, 1, stride=1, stride_axis=0).astype(BF)


def forward_body(
    idx, x, near, far, ta, g0, g1, g2, g3, mix, yt, keep, send, basis, gt, ws
):
    ch = idx[0]
    first = idx[1] == 0

    def row(m, at):
        if REACH <= m < REACH + ROWS:
            return x[m - REACH, pl.ds(at, SPAN), :]
        n = m if m < REACH else m - REACH - ROWS
        a = near[n, pl.ds(at, SPAN), :]
        b = far[n, pl.ds(at, SPAN), :]
        return jnp.where(first, b, a) if m < REACH else jnp.where(first, a, b)

    zeros = jnp.zeros((256 - NSP * SPAN, C), BF)

    @pl.loop(0, WIN // BLK)
    def _(b):
        at = pl.multiple_of(b * BLK, BLK)
        rows = [row(m, at) for m in range(ROWS + 2 * REACH)]
        for i in range(ROWS):
            rhs = jnp.concatenate(rows[i : i + NSP] + [zeros], axis=0)
            out = jnp.dot(ta[i], rhs, preferred_element_type=F32).astype(BF)
            for k in range(K):
                basis[pl.ds(pl.multiple_of(i * WIN + at, BLK), BLK), k * C : (k + 1) * C] = out[k * BLK : (k + 1) * BLK]

    m = mix[...]
    for i in range(ROWS):
        y = jnp.dot(basis[i * WIN : (i + 1) * WIN, :], m, preferred_element_type=F32)
        yt[i] = y.T.astype(BF)

    gather_parts(ch, (g0, g1, g2, g3), 0, gt)
    lane = lax.broadcasted_iota(jnp.int32, (C, WIN), 1)
    own = (lane >= G_OFF) & (lane < G_OFF + PART)
    g = jnp.concatenate([jnp.where(own, gt[r].astype(F32), 0.0).astype(BF) for r in range(ROWS)], axis=1)
    low = lax.broadcasted_iota(jnp.int32, (32, 8, C), 1) < 4

    def weight(k):
        return jnp.dot(g, basis[:, k * C : (k + 1) * C], preferred_element_type=F32).T.reshape(32, 8, C)

    for m in range(5):
        wa = weight(2 * m)
        wb = weight(2 * m + 1) if 2 * m + 1 < K else wa
        even = jnp.where(low, wa, pltpu.roll(wb, 4, 1))
        odd = jnp.where(low, pltpu.roll(wa, 4, 1), wb)
        keep[:, 8 * m : 8 * m + 8, :] = jnp.where(first, even, odd)
        ws[:, 8 * m : 8 * m + 8, :] = jnp.where(first, odd, even)
    send[...] = ws[...].reshape(32 * 40, C).astype(BF)


def backward_body(idx, g0, g1, g2, g3, tb, mix, mid, near, far, gt, bg, rim):
    gather_parts(idx[0], (g0, g1, g2, g3), 0, gt)
    bg[:, WIN:, :] = jnp.zeros((ROWS, PAD - WIN, K * C), BF)
    for i in range(ROWS):
        g = gt[i].T
        for k in range(K):
            bg[i, :WIN, k * C : (k + 1) * C] = lax.dot_general(
                g, mix[k * C : (k + 1) * C, :], (((1,), (1,)), ((), ())), preferred_element_type=F32
            ).astype(BF)
    zeros = jnp.zeros((512 - K * SPAN, C), BF)

    @pl.loop(0, WIN // BLK)
    def _(b):
        at = pl.multiple_of(b * BLK, BLK)
        acc = [None] * (ROWS + 2 * REACH)
        for i in range(ROWS):
            rhs = jnp.concatenate(
                [bg[i, pl.ds(at, SPAN), k * C : (k + 1) * C] for k in range(K)] + [zeros], axis=0
            )
            out = jnp.dot(tb[i], rhs, preferred_element_type=F32)
            for sp in range(NSP):
                part = out[sp * BLK : (sp + 1) * BLK]
                acc[i + sp] = part if acc[i + sp] is None else acc[i + sp] + part
        for n in range(2):
            rim[0, n, pl.ds(at, BLK), :] = acc[n].astype(BF)
            rim[1, n, pl.ds(at, BLK), :] = acc[ROWS + REACH + n].astype(BF)
        for n in range(ROWS):
            mid[n, pl.ds(at, BLK), :] = acc[REACH + n]

    near[...] = rim[1 - idx[1]]
    far[...] = rim[idx[1]]


def join_body(idx, mid, near, far, yt, o0, o1, o2, o3, rest, scr):
    first = idx[1] == 0
    for r in range(ROWS):
        v = mid[r]
        if r < REACH:
            v = v + jnp.where(first, far[r], near[r]).astype(F32)
        if r >= ROWS - REACH:
            n = r - (ROWS - REACH)
            v = v + jnp.where(first, near[n], far[n]).astype(F32)
        if r < ROWS - LATE:
            scr[r] = v.T.astype(BF)
        else:
            rest[r - (ROWS - LATE)] = v.T.astype(BF)
    for s, o in enumerate((o0, o1, o2, o3)):
        to = lax.bitwise_xor(idx[0], jnp.int32(s))
        at = pl.ds(pl.multiple_of(to * OWN, OWN), OWN)
        o[:ROWS] = yt[:, at, :]
        o[ROWS:] = scr[:, at, :]


def fold_lat_body(idx, got, rest, o0, o1, o2, o3, ws):
    total = jnp.sum(got[...].astype(F32).reshape(32, 40, C), axis=0)
    for h in range(4):
        cols = total[:, h * OWN : (h + 1) * OWN]
        v = jnp.concatenate([cols[8 * m : 8 * m + 8] for m in range(5)] + [jnp.zeros((8, OWN), F32)], axis=1)
        high = v.astype(BF).astype(F32)
        ws[h] = jnp.concatenate([high, v - high], axis=0).astype(BF)
    for s, o in enumerate((o0, o1, o2, o3)):
        to = lax.bitwise_xor(idx[0], jnp.int32(s))
        for r in range(LATE):
            o[r * OWN : (r + 1) * OWN, :] = rest[r, pl.ds(pl.multiple_of(to * OWN, OWN), OWN), :]
        o[LATE * OWN :, :] = ws[to]


def unpack_body(scale, idx, a0, a1, a2, a3, b0, b1, b2, b3, y, g, w, sa, sb):
    for s, (a, b) in enumerate(((a0, b0), (a1, b1), (a2, b2), (a3, b3))):
        src = lax.bitwise_xor(idx[0], jnp.int32(s))
        sa[src] = a[...]
        sb[src] = b[...]
    for r in range(ROWS):
        y[r] = jnp.concatenate([sa[h, r][:, G_OFF : G_OFF + PART] for h in range(4)], axis=1)
    for r in range(ROWS - LATE):
        g[r] = jnp.concatenate([sa[h, ROWS + r][:, :PART] for h in range(4)], axis=1)
    for r in range(LATE):
        g[ROWS - LATE + r] = jnp.concatenate([sb[h, r * OWN : (r + 1) * OWN, :PART] for h in range(4)], axis=1)
    total = jnp.zeros((8, WIN), F32)
    for h in range(4):
        v = sb[h, LATE * OWN :, :].astype(F32)
        total = total + (v[:8] + v[8:])
    total = total * scale
    for k in range(K):
        m, odd = divmod(k, 2)
        for r in range(4):
            row = 4 * odd + r
            w[r, k : k + 1, :] = total[row : row + 1, m * OWN : (m + 1) * OWN]


def fold_core_body(idx, keep, got, out):
    out[...] = (keep[...] + got[...].astype(F32)).astype(BF)


def swap_ch(mask):
    return [(i, i ^ mask) for i in range(4)]


def swap_lat():
    near = [(i, i ^ 1) for i in range(64)]
    far = []
    for i in range(1, 63, 2):
        far += [(i, i + 1), (i + 1, i)]
    return near, far


def local(x_field, cotangent, halo_rows, filters, mixing):
    lat = lax.axis_index("lat")
    ch = lax.axis_index("ch")
    idx = jnp.stack([ch, lat % 2]).astype(jnp.int32)
    mix2 = mixing.reshape(K * C, C)
    pair = ((2 * ROWS, OWN, WIN), BF)

    def exchange(parts):
        got = {s: lax.ppermute(parts[s], "ch", swap_ch(s)) for s in (2, 1, 3)}
        return [parts[0], got[1], got[2], got[3]]

    parts = exchange(
        call(pack_body, "pack", [pair] * 4, 2, [pltpu.VMEM((4, 2 * ROWS, OWN, WIN), BF)])(idx, cotangent, x_field)
    )

    want = lat * ROWS + jnp.arange(ROWS, dtype=jnp.int32)[:, None] - REACH + jnp.arange(NSP, dtype=jnp.int32)[None, :]
    hit = (halo_rows[:, :, None] == want[:, None, :]) & (halo_rows[:, :, None] >= 0)
    taps = jnp.sum(jnp.where(hit[:, :, None, :, None], filters.astype(F32)[:, :, :, None, :], 0.0), axis=1)
    ntap = taps.shape[-1]
    a = jnp.pad(taps, ((0, 0),) * 3 + ((0, SPAN - ntap),)).reshape(ROWS * K, NSP * SPAN)
    a = jnp.pad(a, ((0, 0), (0, 256 - NSP * SPAN)))
    b = jnp.pad(taps[..., ::-1], ((0, 0),) * 3 + ((1, SPAN - ntap - 1),))
    b = jnp.transpose(b, (0, 2, 1, 3)).reshape(ROWS * NSP, K * SPAN)
    b = jnp.pad(b, ((0, 0), (0, 512 - K * SPAN)))
    ta, tb = call(
        bands_body, "bands", [((ROWS, K * BLK, 256), BF), ((ROWS, NSP * BLK, 512), BF)], 2
    )(idx, a, b)

    parts, ta, tb = lax.optimization_barrier((parts, ta, tb))
    lon = (ROWS, PAD, C)
    rim = (REACH, PAD, C)
    x_lon, x_near, x_far = call(
        asm_x_body, "asm_x", [(lon, BF), (rim, BF), (rim, BF)], 4, [pltpu.VMEM((ROWS, C, WIN), BF)]
    )(idx, *parts)
    to_near, to_far = swap_lat()
    x_far = lax.ppermute(x_far, "lat", to_far)
    x_near = lax.ppermute(x_near, "lat", to_near)

    tb, _ = lax.optimization_barrier((tb, x_lon))
    mid, near, far = call(
        backward_body,
        "backward",
        [((ROWS, WIN, C), F32), ((REACH, WIN, C), BF), ((REACH, WIN, C), BF)],
        6,
        [
            pltpu.VMEM((ROWS, C, WIN), BF),
            pltpu.VMEM((ROWS, PAD, K * C), BF),
            pltpu.VMEM((2, REACH, WIN, C), BF),
        ],
        limit=20,
        flops=8_000_000_000,
        nbytes=5_000_000,
    )(idx, *parts, tb, mix2)
    far = lax.ppermute(far, "lat", to_far)
    near = lax.ppermute(near, "lat", to_near)

    ta, mid = lax.optimization_barrier((ta, mid))
    yt, keep, send = call(
        forward_body,
        "forward",
        [((ROWS, C, WIN), BF), ((32, 40, C), F32), ((32 * 40, C), BF)],
        9,
        [pltpu.VMEM((ROWS * WIN, K * C), BF), pltpu.VMEM((ROWS, C, WIN), BF), pltpu.VMEM((32, 40, C), F32)],
        limit=28,
        flops=8_000_000_000,
        nbytes=9_000_000,
    )(idx, x_lon, x_near, x_far, ta, *parts, mix2)
    yt, send, near, far = lax.optimization_barrier((yt, send, near, far))
    got = lax.ppermute(send, "lat", to_near)
    early = ((2 * ROWS - LATE, OWN, WIN), BF)
    late = (LATE * OWN + 16, WIN)
    *outs, rest = call(
        join_body, "join", [early] * 4 + [((LATE, C, WIN), BF)], 4, [pltpu.VMEM((ROWS - LATE, C, WIN), BF)], limit=10
    )(idx, mid, near, far, yt)
    got, _ = lax.optimization_barrier((got, outs[0]))
    outs = exchange(outs)
    (half,) = call(fold_core_body, "fold_core", [((32 * 40, C), BF)], 2)(idx, keep.reshape(32 * 40, C), got)
    groups = [[2 * q + core for q in range(32)] for core in range(2)]
    got = lax.all_to_all(half, "lat", 0, 0, axis_index_groups=groups, tiled=True)
    last = exchange(call(fold_lat_body, "fold_lat", [(late, BF)] * 4, 2, [pltpu.VMEM((4, 16, WIN), BF)])(idx, got, rest))
    return call(
        functools.partial(unpack_body, 1.0 / math.sqrt(64 * ROWS * J)),
        "unpack",
        [((ROWS, OWN, J), BF), ((ROWS, OWN, J), BF), ((4, K, OWN), F32)],
        8,
        [pltpu.VMEM((4, 2 * ROWS - LATE, OWN, WIN), BF), pltpu.VMEM((4,) + late, BF)],
    )(idx, *outs, *last)


def solution(mesh):
    return jax.shard_map(
        local,
        mesh=mesh,
        in_specs=(
            P("lat", "ch", None),
            P("lat", "ch", None),
            P("lat", None),
            P("lat", None, None, None),
            P(),
        ),
        out_specs=(P("lat", "ch", None), P("lat", "ch", None), P("lat", None, "ch")),
        check_vma=False,
    )
```

```python
import functools
import math

import jax
import jax.numpy as jnp
from jax import lax
from jax.experimental import pallas as pl
from jax.experimental.pallas import tpu as pltpu
from jax.sharding import PartitionSpec as P

BF = jnp.bfloat16
F32 = jnp.float32
ROWS = 3
OWN = 64
C = 256
J = 1440
K = 9
PART = 360
WIN = 384
PAD = 400
BLK = 32
SPAN = 48
REACH = 2
NSP = 5
X_OFF = 16
G_OFF = 8
LATE = 1
MIB = 1024 * 1024

VM = pl.BlockSpec(memory_space=pltpu.VMEM)
SM = pl.BlockSpec(memory_space=pltpu.SMEM)


def call(body, name, outs, n_in, scratch=(), limit=8, flops=0, nbytes=1_000_000):
    return pl.pallas_call(
        body,
        out_shape=[jax.ShapeDtypeStruct(s, d) for s, d in outs],
        in_specs=[SM] + [VM] * n_in,
        out_specs=[VM] * len(outs),
        scratch_shapes=list(scratch),
        compiler_params=pltpu.CompilerParams(vmem_limit_bytes=limit * MIB),
        cost_estimate=pl.CostEstimate(flops=flops, bytes_accessed=nbytes, transcendentals=0),
        name=name,
    )


def pack_body(idx, g, x, o0, o1, o2, o3, win):
    for r in range(2 * ROWS):
        v = g[r] if r < ROWS else x[r - ROWS]
        for h in range(4):
            a = PART * h - (G_OFF if r < ROWS else X_OFF)
            if a < 0:
                w = jnp.concatenate([v[:, J + a :], v[:, : WIN + a]], axis=1)
            elif a + WIN > J:
                w = jnp.concatenate([v[:, a:], v[:, : a + WIN - J]], axis=1)
            else:
                w = v[:, a : a + WIN]
            win[h, r] = w
    for s, o in enumerate((o0, o1, o2, o3)):
        o[...] = win[lax.bitwise_xor(idx[0], jnp.int32(s))]


def gather_parts(ch, refs, first, scr):
    for s, ref in enumerate(refs):
        src = lax.bitwise_xor(ch, jnp.int32(s))
        scr[:, pl.ds(pl.multiple_of(src * OWN, OWN), OWN), :] = ref[first : first + ROWS]


def asm_x_body(idx, p0, p1, p2, p3, out, near, far, scr):
    gather_parts(idx[0], (p0, p1, p2, p3), ROWS, scr)
    zeros = jnp.zeros((PAD - WIN, C), BF)
    for r in range(ROWS):
        out[r, :WIN, :] = scr[r].T
        out[r, WIN:, :] = zeros

    @pl.when(idx[1] == 0)
    def _():
        near[...] = out[1:]
        far[...] = out[:REACH]

    @pl.when(idx[1] != 0)
    def _():
        near[...] = out[:REACH]
        far[...] = out[1:]


def bands_body(idx, a, b, ta, tb):
    for n in range(ROWS * K):
        i, k = divmod(n, K)
        row = jnp.broadcast_to(a[n : n + 1, :], (BLK, 256))
        ta[i, k * BLK : (k + 1) * BLK, :] = pltpu.roll(row, 0, 1, stride=1, stride_axis=0).astype(BF)
    for n in range(ROWS * NSP):
        i, sp = divmod(n, NSP)
        row = jnp.broadcast_to(b[n : n + 1, :], (BLK, 512))
        tb[i, sp * BLK : (sp + 1) * BLK, :] = pltpu.roll(row, 0, 1, stride=1, stride_axis=0).astype(BF)


def forward_body(
    idx, x, near, far, ta, g0, g1, g2, g3, mix, yt, keep, send, basis, gt, ws
):
    ch = idx[0]
    first = idx[1] == 0

    def row(m, at):
        if REACH <= m < REACH + ROWS:
            return x[m - REACH, pl.ds(at, SPAN), :]
        n = m if m < REACH else m - REACH - ROWS
        a = near[n, pl.ds(at, SPAN), :]
        b = far[n, pl.ds(at, SPAN), :]
        return jnp.where(first, b, a) if m < REACH else jnp.where(first, a, b)

    zeros = jnp.zeros((256 - NSP * SPAN, C), BF)

    @pl.loop(0, WIN // BLK)
    def _(b):
        at = pl.multiple_of(b * BLK, BLK)
        rows = [row(m, at) for m in range(ROWS + 2 * REACH)]
        for i in range(ROWS):
            rhs = jnp.concatenate(rows[i : i + NSP] + [zeros], axis=0)
            out = jnp.dot(ta[i], rhs, preferred_element_type=F32).astype(BF)
            for k in range(K):
                basis[pl.ds(pl.multiple_of(i * WIN + at, BLK), BLK), k * C : (k + 1) * C] = out[k * BLK : (k + 1) * BLK]

    m = mix[...]
    for i in range(ROWS):
        y = jnp.dot(basis[i * WIN : (i + 1) * WIN, :], m, preferred_element_type=F32)
        yt[i] = y.T.astype(BF)

    gather_parts(ch, (g0, g1, g2, g3), 0, gt)
    lane = lax.broadcasted_iota(jnp.int32, (C, WIN), 1)
    own = (lane >= G_OFF) & (lane < G_OFF + PART)
    g = jnp.concatenate([jnp.where(own, gt[r].astype(F32), 0.0).astype(BF) for r in range(ROWS)], axis=1)
    low = lax.broadcasted_iota(jnp.int32, (32, 8, C), 1) < 4

    def weight(k):
        return jnp.dot(g, basis[:, k * C : (k + 1) * C], preferred_element_type=F32).T.reshape(32, 8, C)

    for m in range(5):
        wa = weight(2 * m)
        wb = weight(2 * m + 1) if 2 * m + 1 < K else wa
        even = jnp.where(low, wa, pltpu.roll(wb, 4, 1))
        odd = jnp.where(low, pltpu.roll(wa, 4, 1), wb)
        keep[:, 8 * m : 8 * m + 8, :] = jnp.where(first, even, odd)
        ws[:, 8 * m : 8 * m + 8, :] = jnp.where(first, odd, even)
    send[...] = ws[...].reshape(32 * 40, C).astype(BF)


def backward_body(idx, g0, g1, g2, g3, tb, mix, mid, near, far, gt, bg, rim):
    gather_parts(idx[0], (g0, g1, g2, g3), 0, gt)
    bg[:, WIN:, :] = jnp.zeros((ROWS, PAD - WIN, K * C), BF)
    for i in range(ROWS):
        g = gt[i].T
        for k in range(K):
            bg[i, :WIN, k * C : (k + 1) * C] = lax.dot_general(
                g, mix[k * C : (k + 1) * C, :], (((1,), (1,)), ((), ())), preferred_element_type=F32
            ).astype(BF)
    zeros = jnp.zeros((512 - K * SPAN, C), BF)

    @pl.loop(0, WIN // BLK)
    def _(b):
        at = pl.multiple_of(b * BLK, BLK)
        acc = [None] * (ROWS + 2 * REACH)
        for i in range(ROWS):
            rhs = jnp.concatenate(
                [bg[i, pl.ds(at, SPAN), k * C : (k + 1) * C] for k in range(K)] + [zeros], axis=0
            )
            out = jnp.dot(tb[i], rhs, preferred_element_type=F32)
            for sp in range(NSP):
                part = out[sp * BLK : (sp + 1) * BLK]
                acc[i + sp] = part if acc[i + sp] is None else acc[i + sp] + part
        for n in range(2):
            rim[0, n, pl.ds(at, BLK), :] = acc[n].astype(BF)
            rim[1, n, pl.ds(at, BLK), :] = acc[ROWS + REACH + n].astype(BF)
        for n in range(ROWS):
            mid[n, pl.ds(at, BLK), :] = acc[REACH + n]

    near[...] = rim[1 - idx[1]]
    far[...] = rim[idx[1]]


def join_body(idx, mid, near, far, yt, o0, o1, o2, o3, rest, scr):
    first = idx[1] == 0
    for r in range(ROWS):
        v = mid[r]
        if r < REACH:
            v = v + jnp.where(first, far[r], near[r]).astype(F32)
        if r >= ROWS - REACH:
            n = r - (ROWS - REACH)
            v = v + jnp.where(first, near[n], far[n]).astype(F32)
        if r < ROWS - LATE:
            scr[r] = v.T.astype(BF)
        else:
            rest[r - (ROWS - LATE)] = v.T.astype(BF)
    for s, o in enumerate((o0, o1, o2, o3)):
        to = lax.bitwise_xor(idx[0], jnp.int32(s))
        at = pl.ds(pl.multiple_of(to * OWN, OWN), OWN)
        o[:ROWS] = yt[:, at, :]
        o[ROWS:] = scr[:, at, :]


def fold_lat_body(idx, got, rest, o0, o1, o2, o3, ws):
    total = jnp.sum(got[...].astype(F32).reshape(32, 40, C), axis=0)
    for h in range(4):
        cols = total[:, h * OWN : (h + 1) * OWN]
        v = jnp.concatenate([cols[8 * m : 8 * m + 8] for m in range(5)] + [jnp.zeros((8, OWN), F32)], axis=1)
        high = v.astype(BF).astype(F32)
        ws[h] = jnp.concatenate([high, v - high], axis=0).astype(BF)
    for s, o in enumerate((o0, o1, o2, o3)):
        to = lax.bitwise_xor(idx[0], jnp.int32(s))
        for r in range(LATE):
            o[r * OWN : (r + 1) * OWN, :] = rest[r, pl.ds(pl.multiple_of(to * OWN, OWN), OWN), :]
        o[LATE * OWN :, :] = ws[to]


def unpack_y_body(idx, a0, a1, a2, a3, y, sa):
    for s, a in enumerate((a0, a1, a2, a3)):
        sa[lax.bitwise_xor(idx[0], jnp.int32(s))] = a[:ROWS]
    for r in range(ROWS):
        y[r] = jnp.concatenate([sa[h, r][:, G_OFF : G_OFF + PART] for h in range(4)], axis=1)


def unpack_g_body(scale, idx, a0, a1, a2, a3, b0, b1, b2, b3, g, w, sa, sb):
    for s, (a, b) in enumerate(((a0, b0), (a1, b1), (a2, b2), (a3, b3))):
        src = lax.bitwise_xor(idx[0], jnp.int32(s))
        sa[src] = a[ROWS:]
        sb[src] = b[...]
    for r in range(ROWS - LATE):
        g[r] = jnp.concatenate([sa[h, r][:, :PART] for h in range(4)], axis=1)
    for r in range(LATE):
        g[ROWS - LATE + r] = jnp.concatenate([sb[h, r * OWN : (r + 1) * OWN, :PART] for h in range(4)], axis=1)
    total = jnp.zeros((8, WIN), F32)
    for h in range(4):
        v = sb[h, LATE * OWN :, :].astype(F32)
        total = total + (v[:8] + v[8:])
    total = total * scale
    for k in range(K):
        m, odd = divmod(k, 2)
        w[k] = total[4 * odd : 4 * odd + 4, m * OWN : (m + 1) * OWN]


def fold_core_body(idx, keep, got, out):
    out[...] = (keep[...] + got[...].astype(F32)).astype(BF)


def swap_ch(mask):
    return [(i, i ^ mask) for i in range(4)]


def swap_lat():
    near = [(i, i ^ 1) for i in range(64)]
    far = []
    for i in range(1, 63, 2):
        far += [(i, i + 1), (i + 1, i)]
    return near, far


def local(x_field, cotangent, halo_rows, filters, mixing):
    lat = lax.axis_index("lat")
    ch = lax.axis_index("ch")
    idx = jnp.stack([ch, lat % 2]).astype(jnp.int32)
    mix2 = mixing.reshape(K * C, C)
    pair = ((2 * ROWS, OWN, WIN), BF)

    def exchange(parts):
        got = {s: lax.ppermute(parts[s], "ch", swap_ch(s)) for s in (2, 1, 3)}
        return [parts[0], got[1], got[2], got[3]]

    parts = exchange(
        call(pack_body, "pack", [pair] * 4, 2, [pltpu.VMEM((4, 2 * ROWS, OWN, WIN), BF)])(idx, cotangent, x_field)
    )

    want = lat * ROWS + jnp.arange(ROWS, dtype=jnp.int32)[:, None] - REACH + jnp.arange(NSP, dtype=jnp.int32)[None, :]
    hit = (halo_rows[:, :, None] == want[:, None, :]) & (halo_rows[:, :, None] >= 0)
    taps = jnp.sum(jnp.where(hit[:, :, None, :, None], filters.astype(F32)[:, :, :, None, :], 0.0), axis=1)
    ntap = taps.shape[-1]
    a = jnp.pad(taps, ((0, 0),) * 3 + ((0, SPAN - ntap),)).reshape(ROWS * K, NSP * SPAN)
    a = jnp.pad(a, ((0, 0), (0, 256 - NSP * SPAN)))
    b = jnp.pad(taps[..., ::-1], ((0, 0),) * 3 + ((1, SPAN - ntap - 1),))
    b = jnp.transpose(b, (0, 2, 1, 3)).reshape(ROWS * NSP, K * SPAN)
    b = jnp.pad(b, ((0, 0), (0, 512 - K * SPAN)))
    ta, tb = call(
        bands_body, "bands", [((ROWS, K * BLK, 256), BF), ((ROWS, NSP * BLK, 512), BF)], 2
    )(idx, a, b)

    parts, ta, tb = lax.optimization_barrier((parts, ta, tb))
    lon = (ROWS, PAD, C)
    rim = (REACH, PAD, C)
    x_lon, x_near, x_far = call(
        asm_x_body, "asm_x", [(lon, BF), (rim, BF), (rim, BF)], 4, [pltpu.VMEM((ROWS, C, WIN), BF)]
    )(idx, *parts)
    to_near, to_far = swap_lat()
    x_far = lax.ppermute(x_far, "lat", to_far)
    x_near = lax.ppermute(x_near, "lat", to_near)

    tb, _ = lax.optimization_barrier((tb, x_lon))
    mid, near, far = call(
        backward_body,
        "backward",
        [((ROWS, WIN, C), F32), ((REACH, WIN, C), BF), ((REACH, WIN, C), BF)],
        6,
        [
            pltpu.VMEM((ROWS, C, WIN), BF),
            pltpu.VMEM((ROWS, PAD, K * C), BF),
            pltpu.VMEM((2, REACH, WIN, C), BF),
        ],
        limit=20,
        flops=8_000_000_000,
        nbytes=5_000_000,
    )(idx, *parts, tb, mix2)
    far = lax.ppermute(far, "lat", to_far)
    near = lax.ppermute(near, "lat", to_near)

    ta, mid = lax.optimization_barrier((ta, mid))
    yt, keep, send = call(
        forward_body,
        "forward",
        [((ROWS, C, WIN), BF), ((32, 40, C), F32), ((32 * 40, C), BF)],
        9,
        [pltpu.VMEM((ROWS * WIN, K * C), BF), pltpu.VMEM((ROWS, C, WIN), BF), pltpu.VMEM((32, 40, C), F32)],
        limit=28,
        flops=8_000_000_000,
        nbytes=9_000_000,
    )(idx, x_lon, x_near, x_far, ta, *parts, mix2)
    yt, send, near, far = lax.optimization_barrier((yt, send, near, far))
    got = lax.ppermute(send, "lat", to_near)
    early = ((2 * ROWS - LATE, OWN, WIN), BF)
    late = (LATE * OWN + 16, WIN)
    *outs, rest = call(
        join_body, "join", [early] * 4 + [((LATE, C, WIN), BF)], 4, [pltpu.VMEM((ROWS - LATE, C, WIN), BF)], limit=10
    )(idx, mid, near, far, yt)
    got, _ = lax.optimization_barrier((got, outs[0]))
    outs = exchange(outs)
    (half,) = call(fold_core_body, "fold_core", [((32 * 40, C), BF)], 2)(idx, keep.reshape(32 * 40, C), got)
    groups = [[2 * q + core for q in range(32)] for core in range(2)]
    got = lax.all_to_all(half, "lat", 0, 0, axis_index_groups=groups, tiled=True)
    last = exchange(call(fold_lat_body, "fold_lat", [(late, BF)] * 4, 2, [pltpu.VMEM((4, 16, WIN), BF)])(idx, got, rest))
    (y_field,) = call(
        unpack_y_body, "unpack_y", [((ROWS, OWN, J), BF)], 4, [pltpu.VMEM((4, ROWS, OWN, WIN), BF)]
    )(idx, *outs)
    last, y_field = lax.optimization_barrier((last, y_field))
    x_grad, w = call(
        functools.partial(unpack_g_body, 1.0 / math.sqrt(64 * ROWS * J)),
        "unpack_g",
        [((ROWS, OWN, J), BF), ((K, 4, OWN), F32)],
        8,
        [pltpu.VMEM((4, ROWS - LATE, OWN, WIN), BF), pltpu.VMEM((4,) + late, BF)],
    )(idx, *outs, *last)
    return (y_field, x_grad, jnp.transpose(w, (1, 0, 2)))


def solution(mesh):
    return jax.shard_map(
        local,
        mesh=mesh,
        in_specs=(
            P("lat", "ch", None),
            P("lat", "ch", None),
            P("lat", None),
            P("lat", None, None, None),
            P(),
        ),
        out_specs=(P("lat", "ch", None), P("lat", "ch", None), P("lat", None, "ch")),
        check_vma=False,
    )
```

```python
import functools
import math

import jax
import jax.numpy as jnp
from jax import lax
from jax.experimental import pallas as pl
from jax.experimental.pallas import tpu as pltpu
from jax.sharding import PartitionSpec as P

BF = jnp.bfloat16
F32 = jnp.float32
ROWS = 3
OWN = 64
C = 256
J = 1440
K = 9
PART = 360
WIN = 384
PAD = 400
BLK = 32
SPAN = 48
REACH = 2
NSP = 5
X_OFF = 16
G_OFF = 8
LATE = 1
MIB = 1024 * 1024

VM = pl.BlockSpec(memory_space=pltpu.VMEM)
SM = pl.BlockSpec(memory_space=pltpu.SMEM)


def call(body, name, outs, n_in, scratch=(), limit=8, flops=0, nbytes=1_000_000):
    return pl.pallas_call(
        body,
        out_shape=[jax.ShapeDtypeStruct(s, d) for s, d in outs],
        in_specs=[SM] + [VM] * n_in,
        out_specs=[VM] * len(outs),
        scratch_shapes=list(scratch),
        compiler_params=pltpu.CompilerParams(vmem_limit_bytes=limit * MIB),
        cost_estimate=pl.CostEstimate(flops=flops, bytes_accessed=nbytes, transcendentals=0),
        name=name,
    )


def pack_body(idx, g, x, o0, o1, o2, o3, win):
    for r in range(2 * ROWS):
        v = g[r] if r < ROWS else x[r - ROWS]
        for h in range(4):
            a = PART * h - (G_OFF if r < ROWS else X_OFF)
            if a < 0:
                w = jnp.concatenate([v[:, J + a :], v[:, : WIN + a]], axis=1)
            elif a + WIN > J:
                w = jnp.concatenate([v[:, a:], v[:, : a + WIN - J]], axis=1)
            else:
                w = v[:, a : a + WIN]
            win[h, r] = w
    for s, o in enumerate((o0, o1, o2, o3)):
        o[...] = win[lax.rem(idx[0] + s, 4)]


def gather_parts(ch, refs, first, scr):
    for s, ref in enumerate(refs):
        src = lax.rem(ch - s + 4, 4)
        scr[:, pl.ds(pl.multiple_of(src * OWN, OWN), OWN), :] = ref[first : first + ROWS]


def asm_x_body(idx, p0, p1, p2, p3, out, near, far, scr):
    gather_parts(idx[0], (p0, p1, p2, p3), ROWS, scr)
    zeros = jnp.zeros((PAD - WIN, C), BF)
    for r in range(ROWS):
        out[r, :WIN, :] = scr[r].T
        out[r, WIN:, :] = zeros

    @pl.when(idx[1] == 0)
    def _():
        near[...] = out[1:]
        far[...] = out[:REACH]

    @pl.when(idx[1] != 0)
    def _():
        near[...] = out[:REACH]
        far[...] = out[1:]


def bands_body(idx, a, b, ta, tb):
    for n in range(ROWS * K):
        i, k = divmod(n, K)
        row = jnp.broadcast_to(a[n : n + 1, :], (BLK, 256))
        ta[i, k * BLK : (k + 1) * BLK, :] = pltpu.roll(row, 0, 1, stride=1, stride_axis=0).astype(BF)
    for n in range(ROWS * NSP):
        i, sp = divmod(n, NSP)
        row = jnp.broadcast_to(b[n : n + 1, :], (BLK, 512))
        tb[i, sp * BLK : (sp + 1) * BLK, :] = pltpu.roll(row, 0, 1, stride=1, stride_axis=0).astype(BF)


def forward_body(
    idx, x, near, far, ta, g0, g1, g2, g3, mix, yt, keep, send, basis, gt, ws
):
    ch = idx[0]
    first = idx[1] == 0

    def row(m, at):
        if REACH <= m < REACH + ROWS:
            return x[m - REACH, pl.ds(at, SPAN), :]
        n = m if m < REACH else m - REACH - ROWS
        a = near[n, pl.ds(at, SPAN), :]
        b = far[n, pl.ds(at, SPAN), :]
        return jnp.where(first, b, a) if m < REACH else jnp.where(first, a, b)

    zeros = jnp.zeros((256 - NSP * SPAN, C), BF)

    @pl.loop(0, WIN // BLK)
    def _(b):
        at = pl.multiple_of(b * BLK, BLK)
        rows = [row(m, at) for m in range(ROWS + 2 * REACH)]
        for i in range(ROWS):
            rhs = jnp.concatenate(rows[i : i + NSP] + [zeros], axis=0)
            out = jnp.dot(ta[i], rhs, preferred_element_type=F32).astype(BF)
            for k in range(K):
                basis[pl.ds(pl.multiple_of(i * WIN + at, BLK), BLK), k * C : (k + 1) * C] = out[k * BLK : (k + 1) * BLK]

    m = mix[...]
    for i in range(ROWS):
        y = jnp.dot(basis[i * WIN : (i + 1) * WIN, :], m, preferred_element_type=F32)
        yt[i] = y.T.astype(BF)

    gather_parts(ch, (g0, g1, g2, g3), 0, gt)
    lane = lax.broadcasted_iota(jnp.int32, (C, WIN), 1)
    own = (lane >= G_OFF) & (lane < G_OFF + PART)
    g = jnp.concatenate([jnp.where(own, gt[r].astype(F32), 0.0).astype(BF) for r in range(ROWS)], axis=1)
    low = lax.broadcasted_iota(jnp.int32, (32, 8, C), 1) < 4

    def weight(k):
        return jnp.dot(g, basis[:, k * C : (k + 1) * C], preferred_element_type=F32).T.reshape(32, 8, C)

    for m in range(5):
        wa = weight(2 * m)
        wb = weight(2 * m + 1) if 2 * m + 1 < K else wa
        even = jnp.where(low, wa, pltpu.roll(wb, 4, 1))
        odd = jnp.where(low, pltpu.roll(wa, 4, 1), wb)
        keep[:, 8 * m : 8 * m + 8, :] = jnp.where(first, even, odd)
        ws[:, 8 * m : 8 * m + 8, :] = jnp.where(first, odd, even)
    send[...] = ws[...].reshape(32 * 40, C).astype(BF)


def backward_body(idx, g0, g1, g2, g3, tb, mix, mid, near, far, gt, bg, rim):
    gather_parts(idx[0], (g0, g1, g2, g3), 0, gt)
    bg[:, WIN:, :] = jnp.zeros((ROWS, PAD - WIN, K * C), BF)
    for i in range(ROWS):
        g = gt[i].T
        for k in range(K):
            bg[i, :WIN, k * C : (k + 1) * C] = lax.dot_general(
                g, mix[k * C : (k + 1) * C, :], (((1,), (1,)), ((), ())), preferred_element_type=F32
            ).astype(BF)
    zeros = jnp.zeros((512 - K * SPAN, C), BF)

    @pl.loop(0, WIN // BLK)
    def _(b):
        at = pl.multiple_of(b * BLK, BLK)
        acc = [None] * (ROWS + 2 * REACH)
        for i in range(ROWS):
            rhs = jnp.concatenate(
                [bg[i, pl.ds(at, SPAN), k * C : (k + 1) * C] for k in range(K)] + [zeros], axis=0
            )
            out = jnp.dot(tb[i], rhs, preferred_element_type=F32)
            for sp in range(NSP):
                part = out[sp * BLK : (sp + 1) * BLK]
                acc[i + sp] = part if acc[i + sp] is None else acc[i + sp] + part
        for n in range(2):
            rim[0, n, pl.ds(at, BLK), :] = acc[n].astype(BF)
            rim[1, n, pl.ds(at, BLK), :] = acc[ROWS + REACH + n].astype(BF)
        for n in range(ROWS):
            mid[n, pl.ds(at, BLK), :] = acc[REACH + n]

    near[...] = rim[1 - idx[1]]
    far[...] = rim[idx[1]]


def join_body(idx, mid, near, far, yt, o0, o1, o2, o3, rest, scr):
    first = idx[1] == 0
    for r in range(ROWS):
        v = mid[r]
        if r < REACH:
            v = v + jnp.where(first, far[r], near[r]).astype(F32)
        if r >= ROWS - REACH:
            n = r - (ROWS - REACH)
            v = v + jnp.where(first, near[n], far[n]).astype(F32)
        if r < ROWS - LATE:
            scr[r] = v.T.astype(BF)
        else:
            rest[r - (ROWS - LATE)] = v.T.astype(BF)
    for s, o in enumerate((o0, o1, o2, o3)):
        to = lax.rem(idx[0] + s, 4)
        at = pl.ds(pl.multiple_of(to * OWN, OWN), OWN)
        o[:ROWS] = yt[:, at, :]
        o[ROWS:] = scr[:, at, :]


def fold_lat_body(idx, got, rest, o0, o1, o2, o3, ws):
    total = jnp.sum(got[...].astype(F32).reshape(32, 40, C), axis=0)
    for h in range(4):
        cols = total[:, h * OWN : (h + 1) * OWN]
        v = jnp.concatenate([cols[8 * m : 8 * m + 8] for m in range(5)] + [jnp.zeros((8, OWN), F32)], axis=1)
        high = v.astype(BF).astype(F32)
        ws[h] = jnp.concatenate([high, v - high], axis=0).astype(BF)
    for s, o in enumerate((o0, o1, o2, o3)):
        to = lax.rem(idx[0] + s, 4)
        for r in range(LATE):
            o[r * OWN : (r + 1) * OWN, :] = rest[r, pl.ds(pl.multiple_of(to * OWN, OWN), OWN), :]
        o[LATE * OWN :, :] = ws[to]


def unpack_y_body(idx, a0, a1, a2, a3, y, sa):
    for s, a in enumerate((a0, a1, a2, a3)):
        sa[lax.rem(idx[0] - s + 4, 4)] = a[:ROWS]
    for r in range(ROWS):
        y[r] = jnp.concatenate([sa[h, r][:, G_OFF : G_OFF + PART] for h in range(4)], axis=1)


def unpack_g_body(scale, idx, a0, a1, a2, a3, b0, b1, b2, b3, g, w, sa, sb):
    for s, (a, b) in enumerate(((a0, b0), (a1, b1), (a2, b2), (a3, b3))):
        src = lax.rem(idx[0] - s + 4, 4)
        sa[src] = a[ROWS:]
        sb[src] = b[...]
    for r in range(ROWS - LATE):
        g[r] = jnp.concatenate([sa[h, r][:, :PART] for h in range(4)], axis=1)
    for r in range(LATE):
        g[ROWS - LATE + r] = jnp.concatenate([sb[h, r * OWN : (r + 1) * OWN, :PART] for h in range(4)], axis=1)
    total = jnp.zeros((8, WIN), F32)
    for h in range(4):
        v = sb[h, LATE * OWN :, :].astype(F32)
        total = total + (v[:8] + v[8:])
    total = total * scale
    for k in range(K):
        m, odd = divmod(k, 2)
        w[k] = total[4 * odd : 4 * odd + 4, m * OWN : (m + 1) * OWN]


def fold_core_body(idx, keep, got, out):
    out[...] = (keep[...] + got[...].astype(F32)).astype(BF)


def ring_ch(step):
    return [(i, (i + step) % 4) for i in range(4)]


def swap_lat():
    near = [(i, i ^ 1) for i in range(64)]
    far = []
    for i in range(1, 63, 2):
        far += [(i, i + 1), (i + 1, i)]
    return near, far


def local(x_field, cotangent, halo_rows, filters, mixing):
    lat = lax.axis_index("lat")
    ch = lax.axis_index("ch")
    idx = jnp.stack([ch, lat % 2]).astype(jnp.int32)
    mix2 = mixing.reshape(K * C, C)
    pair = ((2 * ROWS, OWN, WIN), BF)

    def exchange(parts):
        got = {s: lax.ppermute(parts[s], "ch", ring_ch(s)) for s in (2, 1, 3)}
        return [parts[0], got[1], got[2], got[3]]

    parts = exchange(
        call(pack_body, "pack", [pair] * 4, 2, [pltpu.VMEM((4, 2 * ROWS, OWN, WIN), BF)])(idx, cotangent, x_field)
    )

    want = lat * ROWS + jnp.arange(ROWS, dtype=jnp.int32)[:, None] - REACH + jnp.arange(NSP, dtype=jnp.int32)[None, :]
    hit = (halo_rows[:, :, None] == want[:, None, :]) & (halo_rows[:, :, None] >= 0)
    taps = jnp.sum(jnp.where(hit[:, :, None, :, None], filters.astype(F32)[:, :, :, None, :], 0.0), axis=1)
    ntap = taps.shape[-1]
    a = jnp.pad(taps, ((0, 0),) * 3 + ((0, SPAN - ntap),)).reshape(ROWS * K, NSP * SPAN)
    a = jnp.pad(a, ((0, 0), (0, 256 - NSP * SPAN)))
    b = jnp.pad(taps[..., ::-1], ((0, 0),) * 3 + ((1, SPAN - ntap - 1),))
    b = jnp.transpose(b, (0, 2, 1, 3)).reshape(ROWS * NSP, K * SPAN)
    b = jnp.pad(b, ((0, 0), (0, 512 - K * SPAN)))
    ta, tb = call(
        bands_body, "bands", [((ROWS, K * BLK, 256), BF), ((ROWS, NSP * BLK, 512), BF)], 2
    )(idx, a, b)

    parts, ta, tb = lax.optimization_barrier((parts, ta, tb))
    lon = (ROWS, PAD, C)
    rim = (REACH, PAD, C)
    x_lon, x_near, x_far = call(
        asm_x_body, "asm_x", [(lon, BF), (rim, BF), (rim, BF)], 4, [pltpu.VMEM((ROWS, C, WIN), BF)]
    )(idx, *parts)
    to_near, to_far = swap_lat()
    x_far = lax.ppermute(x_far, "lat", to_far)
    x_near = lax.ppermute(x_near, "lat", to_near)

    tb, _ = lax.optimization_barrier((tb, x_lon))
    mid, near, far = call(
        backward_body,
        "backward",
        [((ROWS, WIN, C), F32), ((REACH, WIN, C), BF), ((REACH, WIN, C), BF)],
        6,
        [
            pltpu.VMEM((ROWS, C, WIN), BF),
            pltpu.VMEM((ROWS, PAD, K * C), BF),
            pltpu.VMEM((2, REACH, WIN, C), BF),
        ],
        limit=20,
        flops=8_000_000_000,
        nbytes=5_000_000,
    )(idx, *parts, tb, mix2)
    far = lax.ppermute(far, "lat", to_far)
    near = lax.ppermute(near, "lat", to_near)

    ta, mid = lax.optimization_barrier((ta, mid))
    yt, keep, send = call(
        forward_body,
        "forward",
        [((ROWS, C, WIN), BF), ((32, 40, C), F32), ((32 * 40, C), BF)],
        9,
        [pltpu.VMEM((ROWS * WIN, K * C), BF), pltpu.VMEM((ROWS, C, WIN), BF), pltpu.VMEM((32, 40, C), F32)],
        limit=28,
        flops=8_000_000_000,
        nbytes=9_000_000,
    )(idx, x_lon, x_near, x_far, ta, *parts, mix2)
    yt, send, near, far = lax.optimization_barrier((yt, send, near, far))
    got = lax.ppermute(send, "lat", to_near)
    early = ((2 * ROWS - LATE, OWN, WIN), BF)
    late = (LATE * OWN + 16, WIN)
    *outs, rest = call(
        join_body, "join", [early] * 4 + [((LATE, C, WIN), BF)], 4, [pltpu.VMEM((ROWS - LATE, C, WIN), BF)], limit=10
    )(idx, mid, near, far, yt)
    got, _ = lax.optimization_barrier((got, outs[0]))
    outs = exchange(outs)
    (half,) = call(fold_core_body, "fold_core", [((32 * 40, C), BF)], 2)(idx, keep.reshape(32 * 40, C), got)
    groups = [[2 * q + core for q in range(32)] for core in range(2)]
    got = lax.all_to_all(half, "lat", 0, 0, axis_index_groups=groups, tiled=True)
    last = exchange(call(fold_lat_body, "fold_lat", [(late, BF)] * 4, 2, [pltpu.VMEM((4, 16, WIN), BF)])(idx, got, rest))
    (y_field,) = call(
        unpack_y_body, "unpack_y", [((ROWS, OWN, J), BF)], 4, [pltpu.VMEM((4, ROWS, OWN, WIN), BF)]
    )(idx, *outs)
    last, y_field = lax.optimization_barrier((last, y_field))
    x_grad, w = call(
        functools.partial(unpack_g_body, 1.0 / math.sqrt(64 * ROWS * J)),
        "unpack_g",
        [((ROWS, OWN, J), BF), ((K, 4, OWN), F32)],
        8,
        [pltpu.VMEM((4, ROWS - LATE, OWN, WIN), BF), pltpu.VMEM((4,) + late, BF)],
    )(idx, *outs, *last)
    return (y_field, x_grad, jnp.transpose(w, (1, 0, 2)))


def solution(mesh):
    return jax.shard_map(
        local,
        mesh=mesh,
        in_specs=(
            P("lat", "ch", None),
            P("lat", "ch", None),
            P("lat", None),
            P("lat", None, None, None),
            P(),
        ),
        out_specs=(P("lat", "ch", None), P("lat", "ch", None), P("lat", None, "ch")),
        check_vma=False,
    )
```
